512 devices in a mesh: sx: 4 (over x), sy: 2 (over core), dict: 64 (over z, y).
Axes of the slice: x: 4, y: 8, z: 8, core: 2. Of those that a mesh axis runs over, the one named last changes fastest.
Arguments:
- patterns: bfloat16 [8, 512, 1600], P('sx', ('sy', 'dict')), may hold values from -12 to 12
- nlpar_weights: float32 [9, 8, 512], P(None, 'sx', ('sy', 'dict')), may hold values from 0.2 to 2
- dictionary: bfloat16 [1600, 180224], P(None, ('sy', 'dict')), as said below
Outputs:
- best_score: float32 [8, 512], P('sx', ('sy', 'dict'))
The draws below stay inside these ranges and needn't reach their ends.
Inputs may be any that keep to these rules, and one draw needn't show every extreme that they name: Each dictionary column has mean zero and unit Euclidean norm over its 1600 pixels, up to rounding to bfloat16.
All inputs are finite; a program needn't handle non-finite values.
Results may differ from the reference program's by a relative error of at most 0.0003.
Values may be sent and summed in bfloat16 or wider, within the bound.
No kernel may reach another device: no remote copies, remote signals or barrier semaphores. Data moves between devices by JAX's collectives and lax.ppermute only.
A program may use at most 64 MiB of HBM per device.

```python
import math
import jax
import jax.numpy as jnp
from jax import lax

PH = 40
PW = 40
PIX = 1600
ROWS = 8
COLS = 512
DICT = 180224


def grain_setup(key):
    template_key, grain_key, place_key = jax.random.split(key, 3)
    count = ROWS * COLS
    templates = jax.random.truncated_normal(template_key, -4.0, 4.0, (count, PIX), jnp.float32)
    grain_of = jax.random.randint(grain_key, (ROWS, COLS), 0, count)
    planted = jax.random.permutation(place_key, DICT)[:count]
    return (templates, grain_of, planted)


def draw_patterns(key, part):
    templates, grain_of, planted = grain_setup(key)
    key = jax.random.fold_in(key, 5)
    amp_key, noise_key = jax.random.split(key)
    oriented = templates[grain_of.reshape(-1)].reshape(ROWS, COLS, PIX)
    amplitude = jnp.exp(jax.random.uniform(amp_key, (ROWS, COLS, 1), jnp.float32, jnp.log(0.3), jnp.log(1.5)))
    noise = jax.random.truncated_normal(noise_key, -4.0, 4.0, (ROWS, COLS, PIX), jnp.float32)
    return jnp.clip(amplitude * oriented + noise, -12.0, 12.0).astype(jnp.bfloat16)


def draw_dictionary(key, part):
    templates, grain_of, planted = grain_setup(key)
    key = jax.random.fold_in(key, 7)
    raw = jax.random.truncated_normal(key, -5.0, 5.0, (PIX, DICT), jnp.float32)
    raw = raw.at[:, planted].set(templates.T)
    centered = raw - jnp.mean(raw, axis=0, keepdims=True)
    length = jnp.sqrt(jnp.sum(centered * centered, axis=0, keepdims=True))
    return (centered / length).astype(jnp.bfloat16)


def block_levels(rng, shape, shards, smallest, top_value):
    factor_of, own = 1.0, jax.random.fold_in(rng, 6)
    for dim, parts in shards:
        steps = jnp.exp(jax.random.uniform(jax.random.fold_in(own, dim), (parts,), jnp.float32, smallest / len(shards), top_value / len(shards)))
        factor_of = factor_of * jnp.repeat(steps, shape[dim] // parts).reshape([-1 if axis == dim else 1 for axis in range(len(shape))])
    return factor_of


def setup_inputs(seed: int = 0) -> dict:
    seeds = jax.random.split(jax.random.key(seed), 4)
    return {
        "patterns": draw_patterns(jax.random.fold_in(seeds[3], 71), 0),
        "nlpar_weights": jnp.clip(jnp.exp(math.log(2.0) - 2.3025851 * jax.random.uniform(seeds[1], (9, ROWS, COLS), jnp.float32) ** block_levels(seeds[1], (9, ROWS, COLS), ((1, 4), (2, 128)), -0.2, 0.2)), 0.2, 2.0),
        "dictionary": draw_dictionary(jax.random.fold_in(seeds[3], 71), 0),
    }


def box_filter(image):
    extra = [(0, 0)] * (image.ndim - 2) + [(2, 2), (2, 2)]
    padded = jnp.pad(image, extra)
    vertical = padded[..., 0:PH, :]
    for offset in range(1, 5):
        vertical = vertical + padded[..., offset:offset + PH, :]
    total = vertical[..., :, 0:PW]
    for offset in range(1, 5):
        total = total + vertical[..., :, offset:offset + PW]
    return total

def normalize(averaged):
    shaped = averaged.reshape(averaged.shape[:-1] + (PH, PW))
    high = shaped - box_filter(shaped) / 25.0
    high = high.reshape(averaged.shape)
    centered = high - lax.optimization_barrier(jnp.mean(high, axis=-1, keepdims=True))
    scale = jnp.sqrt(lax.optimization_barrier(jnp.mean(centered * centered, axis=-1, keepdims=True)) + 1e-06)
    return (centered / scale).astype(jnp.bfloat16)

def reference(patterns, nlpar_weights, dictionary):
    padded = jnp.pad(patterns.astype(jnp.float32), ((1, 1), (1, 1), (0, 0)))
    inside = jnp.pad(jnp.ones((ROWS, COLS), jnp.float32), ((1, 1), (1, 1)))
    total = jnp.zeros((ROWS, COLS, PIX), jnp.float32)
    weight_sum = jnp.zeros((ROWS, COLS), jnp.float32)
    for row_step in range(3):
        for col_step in range(3):
            index = 3 * row_step + col_step
            weight = nlpar_weights[index] * inside[row_step:row_step + ROWS, col_step:col_step + COLS]
            total = total + weight[:, :, None] * padded[row_step:row_step + ROWS, col_step:col_step + COLS, :]
            weight_sum = weight_sum + weight
    averaged = total / weight_sum[:, :, None]
    normalized = normalize(averaged)

    def row_best(row_block):
        scores = jnp.dot(row_block, dictionary, preferred_element_type=jnp.float32)
        return lax.optimization_barrier(jnp.max(scores, axis=1))
    return lax.map(row_best, normalized)
```

```python
import jax
import jax.numpy as jnp
from jax import lax
from jax.experimental import pallas as pl
from jax.experimental.pallas import tpu as pltpu
from jax.sharding import Mesh
from jax.sharding import PartitionSpec as P

PH = 40
PW = 40
PIX = PH * PW
WIDE = 1792
COLS = ("sy", "z", "y")


def average_kernel(own_ref, low_ref, high_ref, above_ref, below_ref, weight_ref, out_ref):
    f32 = jnp.float32
    lines = [above_ref[0].astype(f32)]
    for row in range(2):
        lines.append(
            jnp.concatenate(
                [
                    low_ref[row].astype(f32)[3:4],
                    own_ref[row].astype(f32),
                    high_ref[row].astype(f32)[0:1],
                ],
                axis=0,
            )
        )
    lines.append(below_ref[0].astype(f32))
    averaged = []
    for row in range(2):
        weight = weight_ref[row]
        total = jnp.zeros((4, PIX), f32)
        for row_step in range(3):
            for col_step in range(3):
                index = 3 * row_step + col_step
                near = lines[row + row_step][col_step : col_step + 4]
                total = total + weight[:, index : index + 1] * near
        averaged.append(total / weight[:, 9:10])
    image = jnp.concatenate(averaged, axis=0)
    image = jnp.concatenate([image, jnp.zeros((8, WIDE - PIX), f32)], axis=1)
    pixel = lax.broadcasted_iota(jnp.int32, (8, WIDE), 1)
    column = pixel % PW
    vertical = image
    for offset in (-2, -1, 1, 2):
        vertical = vertical + pltpu.roll(image, (-offset * PW) % WIDE, 1)
    box = vertical
    for offset in (-2, -1, 1, 2):
        inside = (column + offset >= 0) & (column + offset < PW)
        box = box + jnp.where(inside, pltpu.roll(vertical, (-offset) % WIDE, 1), 0.0)
    high = jnp.where(pixel < PIX, image - box / 25.0, 0.0)
    mean = jnp.sum(high, axis=1, keepdims=True) / PIX
    centered = jnp.where(pixel < PIX, high - mean, 0.0)
    scale = jnp.sqrt(jnp.sum(centered * centered, axis=1, keepdims=True) / PIX + 1e-06)
    out_ref[...] = (centered / scale)[:, :PIX].astype(jnp.bfloat16)


def average(own, low, high, above, below, weights):
    return pl.pallas_call(
        average_kernel,
        out_shape=jax.ShapeDtypeStruct((8, PIX), jnp.bfloat16),
        in_specs=[pl.BlockSpec(memory_space=pltpu.VMEM)] * 6,
        out_specs=pl.BlockSpec(memory_space=pltpu.VMEM),
        compiler_params=pltpu.CompilerParams(vmem_limit_bytes=16 * 1024 * 1024),
        cost_estimate=pl.CostEstimate(flops=1000000, bytes_accessed=200000, transcendentals=0),
    )(own, low, high, above, below, weights)


CHUNKS = [(0, 384), (384, 384), (768, 384), (1152, 256)]


def best_kernel(first_ref, second_ref, own_ref, partner_ref, out_ref, held, sems):
    copies = []
    for side, source in enumerate((own_ref, partner_ref)):
        for part, (start, size) in enumerate(CHUNKS):
            columns = pl.ds(start, size)
            copy = pltpu.make_async_copy(
                source.at[:, columns], held.at[side, :, columns], sems.at[side, part]
            )
            copy.start()
            copies.append((copy, side, start, size))
    points = jnp.concatenate([first_ref[...], second_ref[...]], axis=0)
    best = jnp.full((256, 128), -jnp.inf, jnp.float32)
    for copy, side, start, size in copies:
        copy.wait()
        scores = jnp.dot(
            points, held[side, :, start : start + size], preferred_element_type=jnp.float32
        )
        for piece in range(0, size, 128):
            best = jnp.maximum(best, scores[:, piece : piece + 128])
    out_ref[...] = jnp.max(best.T, axis=0, keepdims=True)


def best_of(first, second, own, partner):
    vmem = pl.BlockSpec(memory_space=pltpu.VMEM)
    whole = pl.BlockSpec(memory_space=pl.ANY)
    return pl.pallas_call(
        best_kernel,
        out_shape=jax.ShapeDtypeStruct((1, 256), jnp.float32),
        in_specs=[vmem, vmem, whole, whole],
        out_specs=vmem,
        scratch_shapes=[
            pltpu.VMEM((2,) + own.shape, own.dtype),
            pltpu.SemaphoreType.DMA((2, len(CHUNKS))),
        ],
        compiler_params=pltpu.CompilerParams(vmem_limit_bytes=24 * 1024 * 1024),
        cost_estimate=pl.CostEstimate(
            flops=2 * 256 * 2 * own.size, bytes_accessed=4 * own.size, transcendentals=0
        ),
    )(first, second, own, partner)


def place(core, z, y):
    return 64 * core + 8 * (z % 8) + y % 8


def parity_class(core, z_odd, y_odd):
    return [place(core, z, y) for z in range(z_odd, 8, 2) for y in range(y_odd, 8, 2)]


PARITIES = [(0, 0), (0, 1), (1, 0), (1, 1)]


def gather_class(block):
    groups = [parity_class(core, z, y) for core in range(2) for z, y in PARITIES]
    copies = jnp.broadcast_to(block[None], (16,) + block.shape)
    got = lax.all_to_all(copies, COLS, 0, 0, axis_index_groups=groups)
    return got.reshape(-1, block.shape[1])


def from_neighbour(block, z_step, y_step):
    pairs = []
    for core, sign in ((0, 1), (1, -1)):
        for z in range(8):
            for y in range(8):
                source = place(core, z + sign * z_step, y + sign * y_step)
                pairs.append((source, place(core, z, y)))
    return lax.ppermute(block, COLS, pairs)


def merge(tables):
    table = jnp.stack([pair.reshape(2, 128) for pair in tables])
    table = jnp.where(lax.axis_index("z") % 2 == 1, table[::-1], table)
    table = jnp.where(lax.axis_index("y") % 2 == 1, table[:, ::-1], table)
    groups = [sum([parity_class(core, z, y) for z, y in PARITIES], []) for core in range(2)]
    shares = lax.all_to_all(table.reshape(64, -1), COLS, 0, 0, axis_index_groups=groups)
    return jnp.max(shares, axis=0)


def rim(patterns):
    last = 63
    at = lax.axis_index(("z", "y"))
    swap = [pair for k in (0, last) for pair in ((k, 64 + k), (64 + k, k))]
    partner = lax.ppermute(patterns, COLS, swap)
    ahead = [(64 * core + k, 64 * core + (k + 1) % 64) for core in range(2) for k in range(64)]
    behind = [(target, source) for source, target in ahead]
    low = lax.ppermute(jnp.where(at == last, partner, patterns), COLS, ahead)
    high = lax.ppermute(jnp.where(at == 0, partner, patterns), COLS, behind)
    lines = [
        jnp.concatenate([low[r : r + 1, 3:], patterns[r : r + 1], high[r : r + 1, :1]], axis=1)
        for r in range(2)
    ]
    down = [(i, i + 1) for i in range(3)]
    above = lax.ppermute(lines[1], "sx", down)
    below = lax.ppermute(lines[0], "sx", [(target, source) for source, target in down])
    return low, high, above, below


def valid_weights(weights, rows, cols):
    row = lax.axis_index("sx") * rows + jnp.arange(rows)
    col = lax.axis_index(COLS) * cols + jnp.arange(cols)
    steps = jnp.arange(-1, 2)
    row_near = row[:, None] + steps
    col_near = col[:, None] + steps
    row_valid = (row_near >= 0) & (row_near < rows * lax.axis_size("sx"))
    col_valid = (col_near >= 0) & (col_near < cols * lax.axis_size(COLS))
    valid = row_valid[:, None, :, None] & col_valid[None, :, None, :]
    kept = jnp.where(valid.reshape(rows, cols, 9), jnp.transpose(weights, (1, 2, 0)), 0.0)
    return jnp.concatenate([kept, jnp.sum(kept, axis=2, keepdims=True)], axis=2)


def on_device(patterns, nlpar_weights, dictionary):
    rows, cols = patterns.shape[:2]
    partner = lax.ppermute(dictionary, "sy", [(0, 1), (1, 0)])
    weights = valid_weights(nlpar_weights, rows, cols)
    normalized = average(patterns, *rim(patterns), weights)
    own = gather_class(normalized)
    ahead = from_neighbour(own, 0, 1)
    across = from_neighbour(own, 1, 0)
    diagonal = from_neighbour(own, 1, 1)
    tables = [
        best_of(own, ahead, dictionary, partner),
        best_of(across, diagonal, dictionary, partner),
    ]
    return merge(tables).reshape(rows, cols)


def solution(mesh):
    split = Mesh(mesh.devices.reshape(4, 2, 8, 8), ("sx",) + COLS)
    return jax.shard_map(
        on_device,
        mesh=split,
        in_specs=(
            P("sx", COLS, None),
            P(None, "sx", COLS),
            P(None, COLS),
        ),
        out_specs=P("sx", COLS),
        check_vma=False,
    )
```

```python
import jax
import jax.numpy as jnp
from jax import lax
from jax.experimental import pallas as pl
from jax.experimental.pallas import tpu as pltpu
from jax.sharding import Mesh
from jax.sharding import PartitionSpec as P

PH = 40
PW = 40
PIX = PH * PW
WIDE = 1792
COLS = ("sy", "z", "y")


def average_kernel(block_ref, low_ref, high_ref, weight_ref, out_ref):
    f32 = jnp.float32
    lines = [
        jnp.concatenate([low_ref[row], block_ref[row], high_ref[row]], axis=0).astype(f32)
        for row in range(4)
    ]
    averaged = []
    for row in range(2):
        weight = weight_ref[row]
        total = jnp.zeros((4, PIX), f32)
        for row_step in range(3):
            for col_step in range(3):
                index = 3 * row_step + col_step
                near = lines[row + row_step][col_step : col_step + 4]
                total = total + weight[:, index : index + 1] * near
        averaged.append(total / weight[:, 9:10])
    image = jnp.concatenate(averaged, axis=0)
    image = jnp.concatenate([image, jnp.zeros((8, WIDE - PIX), f32)], axis=1)
    pixel = lax.broadcasted_iota(jnp.int32, (8, WIDE), 1)
    column = pixel % PW
    vertical = image
    for offset in (-2, -1, 1, 2):
        vertical = vertical + pltpu.roll(image, (-offset * PW) % WIDE, 1)
    box = vertical
    for offset in (-2, -1, 1, 2):
        inside = (column + offset >= 0) & (column + offset < PW)
        box = box + jnp.where(inside, pltpu.roll(vertical, (-offset) % WIDE, 1), 0.0)
    high = jnp.where(pixel < PIX, image - box / 25.0, 0.0)
    mean = jnp.sum(high, axis=1, keepdims=True) / PIX
    centered = jnp.where(pixel < PIX, high - mean, 0.0)
    scale = jnp.sqrt(jnp.sum(centered * centered, axis=1, keepdims=True) / PIX + 1e-06)
    out_ref[...] = (centered / scale)[:, :PIX].astype(jnp.bfloat16)


def average(block, low, high, weights):
    return pl.pallas_call(
        average_kernel,
        out_shape=jax.ShapeDtypeStruct((8, PIX), jnp.bfloat16),
        in_specs=[pl.BlockSpec(memory_space=pltpu.VMEM)] * 4,
        out_specs=pl.BlockSpec(memory_space=pltpu.VMEM),
        compiler_params=pltpu.CompilerParams(vmem_limit_bytes=16 * 1024 * 1024),
        cost_estimate=pl.CostEstimate(flops=1000000, bytes_accessed=200000, transcendentals=0),
    )(block, low, high, weights)


def hold_kernel(own_ref, partner_ref, own_held, partner_held, sems):
    copies = [
        pltpu.make_async_copy(own_ref, own_held, sems.at[0]),
        pltpu.make_async_copy(partner_ref, partner_held, sems.at[1]),
    ]
    for copy in copies:
        copy.start()
    for copy in copies:
        copy.wait()


def hold(own, partner):
    return pl.pallas_call(
        hold_kernel,
        out_shape=[pltpu.VMEM(half.shape, half.dtype) for half in (own, partner)],
        in_specs=[pl.BlockSpec(memory_space=space) for space in (pltpu.HBM, pl.ANY)],
        out_specs=[pl.BlockSpec(memory_space=pltpu.VMEM)] * 2,
        scratch_shapes=[pltpu.SemaphoreType.DMA((2,))],
        compiler_params=pltpu.CompilerParams(vmem_limit_bytes=16 * 1024 * 1024),
        cost_estimate=pl.CostEstimate(
            flops=0, bytes_accessed=2 * 4 * own.size, transcendentals=0
        ),
    )(pltpu.with_memory_space_constraint(own, pltpu.HBM), partner)


def row_best(points, half):
    scores = jnp.dot(points, half, preferred_element_type=jnp.float32)
    return jnp.max(scores, axis=1)


def best_of(first, second, halves):
    points = jnp.concatenate([first, second], axis=0)
    return jnp.maximum(*[row_best(points, half) for half in halves])


def place(core, z, y):
    return 64 * core + 8 * (z % 8) + y % 8


def parity_class(core, z_odd, y_odd):
    return [place(core, z, y) for z in range(z_odd, 8, 2) for y in range(y_odd, 8, 2)]


PARITIES = [(0, 0), (0, 1), (1, 0), (1, 1)]


def gather_class(block):
    groups = [parity_class(core, z, y) for core in range(2) for z, y in PARITIES]
    copies = jnp.broadcast_to(block[None], (16,) + block.shape)
    got = lax.all_to_all(copies, COLS, 0, 0, axis_index_groups=groups)
    return got.reshape(-1, block.shape[1])


def from_neighbour(block, z_step, y_step):
    pairs = []
    for core, sign in ((0, 1), (1, -1)):
        for z in range(8):
            for y in range(8):
                source = place(core, z + sign * z_step, y + sign * y_step)
                pairs.append((source, place(core, z, y)))
    return lax.ppermute(block, COLS, pairs)


def merge(tables):
    table = jnp.stack([pair.reshape(2, 128) for pair in tables])
    table = jnp.where(lax.axis_index("z") % 2 == 1, table[::-1], table)
    table = jnp.where(lax.axis_index("y") % 2 == 1, table[:, ::-1], table)
    groups = [sum([parity_class(core, z, y) for z, y in PARITIES], []) for core in range(2)]
    shares = lax.all_to_all(table.reshape(64, -1), COLS, 0, 0, axis_index_groups=groups)
    return jnp.max(shares, axis=0)


def rim(patterns):
    count = lax.axis_size(COLS)
    down = [(i, i + 1) for i in range(3)]
    up = [(target, source) for source, target in down]
    below = lax.ppermute(patterns, "sx", up)[:1]
    above = lax.ppermute(patterns, "sx", down)[1:]
    block = jnp.concatenate([above, patterns, below], axis=0)
    ahead = [(i, i + 1) for i in range(count - 1)]
    behind = [(target, source) for source, target in ahead]
    low = lax.ppermute(block[:, 3:4], COLS, ahead)
    high = lax.ppermute(block[:, 0:1], COLS, behind)
    return block, low, high


def valid_weights(weights, rows, cols):
    row = lax.axis_index("sx") * rows + jnp.arange(rows)
    col = lax.axis_index(COLS) * cols + jnp.arange(cols)
    steps = jnp.arange(-1, 2)
    row_near = row[:, None] + steps
    col_near = col[:, None] + steps
    row_valid = (row_near >= 0) & (row_near < rows * lax.axis_size("sx"))
    col_valid = (col_near >= 0) & (col_near < cols * lax.axis_size(COLS))
    valid = row_valid[:, None, :, None] & col_valid[None, :, None, :]
    kept = jnp.where(valid.reshape(rows, cols, 9), jnp.transpose(weights, (1, 2, 0)), 0.0)
    return jnp.concatenate([kept, jnp.sum(kept, axis=2, keepdims=True)], axis=2)


def on_device(patterns, nlpar_weights, dictionary):
    rows, cols = patterns.shape[:2]
    shared, patterns = lax.optimization_barrier((dictionary, patterns))
    partner = lax.ppermute(shared, "sy", [(0, 1), (1, 0)])
    weights = valid_weights(nlpar_weights, rows, cols)
    normalized = average(*rim(patterns), weights)
    own = gather_class(normalized)
    ahead = from_neighbour(own, 0, 1)
    across = from_neighbour(own, 1, 0)
    diagonal = from_neighbour(own, 1, 1)
    ahead, *halves = lax.optimization_barrier((ahead, dictionary, partner))
    halves = hold(*halves)
    early = best_of(own, ahead, halves)
    early, across, diagonal = lax.optimization_barrier((early, across, diagonal))
    tables = [early, best_of(across, diagonal, halves)]
    return merge(tables).reshape(rows, cols)


def solution(mesh):
    split = Mesh(mesh.devices.reshape(4, 2, 8, 8), ("sx",) + COLS)
    return jax.shard_map(
        on_device,
        mesh=split,
        in_specs=(
            P("sx", COLS, None),
            P(None, "sx", COLS),
            P(None, COLS),
        ),
        out_specs=P("sx", COLS),
        check_vma=False,
    )
```

```python
import jax
import jax.numpy as jnp
from jax import lax
from jax.experimental import pallas as pl
from jax.experimental.pallas import tpu as pltpu
from jax.sharding import Mesh
from jax.sharding import PartitionSpec as P

PH = 40
PW = 40
PIX = PH * PW
WIDE = 1792
COLS = ("sy", "z", "y")


def average_kernel(block_ref, far_ref, near_ref, weight_ref, out_ref):
    f32 = jnp.float32
    even = weight_ref[0, 0:1, 10:11] > 0.0
    lines = []
    for row in range(4):
        far, near = far_ref[row].astype(f32), near_ref[row].astype(f32)
        sides = jnp.where(even, far, near), jnp.where(even, near, far)
        lines.append(jnp.concatenate([sides[0], block_ref[row].astype(f32), sides[1]], axis=0))
    averaged = []
    for row in range(2):
        weight = weight_ref[row]
        total = jnp.zeros((4, PIX), f32)
        for row_step in range(3):
            for col_step in range(3):
                index = 3 * row_step + col_step
                near = lines[row + row_step][col_step : col_step + 4]
                total = total + weight[:, index : index + 1] * near
        averaged.append(total / weight[:, 9:10])
    image = jnp.concatenate(averaged, axis=0)
    image = jnp.concatenate([image, jnp.zeros((8, WIDE - PIX), f32)], axis=1)
    pixel = lax.broadcasted_iota(jnp.int32, (8, WIDE), 1)
    column = pixel % PW
    vertical = image
    for offset in (-2, -1, 1, 2):
        vertical = vertical + pltpu.roll(image, (-offset * PW) % WIDE, 1)
    box = vertical
    for offset in (-2, -1, 1, 2):
        inside = (column + offset >= 0) & (column + offset < PW)
        box = box + jnp.where(inside, pltpu.roll(vertical, (-offset) % WIDE, 1), 0.0)
    high = jnp.where(pixel < PIX, image - box / 25.0, 0.0)
    mean = jnp.sum(high, axis=1, keepdims=True) / PIX
    centered = jnp.where(pixel < PIX, high - mean, 0.0)
    scale = jnp.sqrt(jnp.sum(centered * centered, axis=1, keepdims=True) / PIX + 1e-06)
    out_ref[...] = (centered / scale)[:, :PIX].astype(jnp.bfloat16)


def average(block, far, near, weights):
    return pl.pallas_call(
        average_kernel,
        out_shape=jax.ShapeDtypeStruct((8, PIX), jnp.bfloat16),
        in_specs=[pl.BlockSpec(memory_space=pltpu.VMEM)] * 4,
        out_specs=pl.BlockSpec(memory_space=pltpu.VMEM),
        compiler_params=pltpu.CompilerParams(vmem_limit_bytes=16 * 1024 * 1024),
        cost_estimate=pl.CostEstimate(flops=1000000, bytes_accessed=200000, transcendentals=0),
    )(block, far, near, weights)


def hold_kernel(own_ref, partner_ref, own_held, partner_held, sems):
    copies = [
        pltpu.make_async_copy(own_ref, own_held, sems.at[0]),
        pltpu.make_async_copy(partner_ref, partner_held, sems.at[1]),
    ]
    for copy in copies:
        copy.start()
    for copy in copies:
        copy.wait()


def hold(own, partner):
    return pl.pallas_call(
        hold_kernel,
        out_shape=[pltpu.VMEM(half.shape, half.dtype) for half in (own, partner)],
        in_specs=[pl.BlockSpec(memory_space=space) for space in (pltpu.HBM, pl.ANY)],
        out_specs=[pl.BlockSpec(memory_space=pltpu.VMEM)] * 2,
        scratch_shapes=[pltpu.SemaphoreType.DMA((2,))],
        compiler_params=pltpu.CompilerParams(vmem_limit_bytes=16 * 1024 * 1024),
        cost_estimate=pl.CostEstimate(
            flops=0, bytes_accessed=2 * 4 * own.size, transcendentals=0
        ),
    )(pltpu.with_memory_space_constraint(own, pltpu.HBM), partner)


def row_best(points, half):
    scores = jnp.dot(points, half, preferred_element_type=jnp.float32)
    return jnp.max(scores, axis=1)


def best_of(first, second, halves):
    points = jnp.concatenate([first, second], axis=0)
    return jnp.maximum(*[row_best(points, half) for half in halves])


def place(core, z, y):
    return 64 * core + 8 * (z % 8) + y % 8


def parity_class(core, z_odd, y_odd):
    return [place(core, z, y) for z in range(z_odd, 8, 2) for y in range(y_odd, 8, 2)]


PARITIES = [(0, 0), (0, 1), (1, 0), (1, 1)]


def gather_class(block):
    groups = [parity_class(core, z, y) for core in range(2) for z, y in PARITIES]
    copies = jnp.broadcast_to(block[None], (16,) + block.shape)
    got = lax.all_to_all(copies, COLS, 0, 0, axis_index_groups=groups)
    return got.reshape(-1, block.shape[1])


def from_neighbour(block, z_step, y_step):
    pairs = []
    for core, sign in ((0, 1), (1, -1)):
        for z in range(8):
            for y in range(8):
                source = place(core, z + sign * z_step, y + sign * y_step)
                pairs.append((source, place(core, z, y)))
    return lax.ppermute(block, COLS, pairs)


def merge(tables):
    table = jnp.stack([pair.reshape(2, 128) for pair in tables])
    table = jnp.where(lax.axis_index("z") % 2 == 1, table[::-1], table)
    table = jnp.where(lax.axis_index("y") % 2 == 1, table[:, ::-1], table)
    groups = [sum([parity_class(core, z, y) for z, y in PARITIES], []) for core in range(2)]
    shares = lax.all_to_all(table.reshape(64, -1), COLS, 0, 0, axis_index_groups=groups)
    return jnp.max(shares, axis=0)


def swap_pairs(starts):
    return [pair for i in starts for pair in ((i, i + 1), (i + 1, i))]


def rim(patterns):
    even = lax.axis_index("sx") % 2 == 0
    near = lax.ppermute(patterns, "sx", swap_pairs((0, 2)))
    far = lax.ppermute(patterns, "sx", swap_pairs((1,)))
    above = jnp.where(even, far[1:], near[1:])
    below = jnp.where(even, near[:1], far[:1])
    block = jnp.concatenate([above, patterns, below], axis=0)
    even = lax.axis_index(COLS) % 2 == 0
    first, last = block[:, 0:1], block[:, 3:4]
    far = lax.ppermute(jnp.where(even, first, last), COLS, swap_pairs(range(1, 127, 2)))
    near = lax.ppermute(jnp.where(even, last, first), COLS, swap_pairs(range(0, 128, 2)))
    return block, far, near


def valid_weights(weights, rows, cols):
    row = lax.axis_index("sx") * rows + jnp.arange(rows)
    col = lax.axis_index(COLS) * cols + jnp.arange(cols)
    steps = jnp.arange(-1, 2)
    row_near = row[:, None] + steps
    col_near = col[:, None] + steps
    row_valid = (row_near >= 0) & (row_near < rows * lax.axis_size("sx"))
    col_valid = (col_near >= 0) & (col_near < cols * lax.axis_size(COLS))
    valid = row_valid[:, None, :, None] & col_valid[None, :, None, :]
    kept = jnp.where(valid.reshape(rows, cols, 9), jnp.transpose(weights, (1, 2, 0)), 0.0)
    total = jnp.sum(kept, axis=2, keepdims=True)
    even = (lax.axis_index(COLS) % 2 == 0).astype(jnp.float32)
    return jnp.concatenate([kept, total, jnp.full_like(total, even)], axis=2)


def on_device(patterns, nlpar_weights, dictionary):
    rows, cols = patterns.shape[:2]
    shared, patterns = lax.optimization_barrier((dictionary, patterns))
    partner = lax.ppermute(shared, "sy", [(0, 1), (1, 0)])
    weights = valid_weights(nlpar_weights, rows, cols)
    normalized = average(*rim(patterns), weights)
    own = gather_class(normalized)
    ahead = from_neighbour(own, 0, 1)
    across = from_neighbour(own, 1, 0)
    diagonal = from_neighbour(own, 1, 1)
    ahead, *halves = lax.optimization_barrier((ahead, dictionary, partner))
    halves = hold(*halves)
    early = best_of(own, ahead, halves)
    early, across, diagonal = lax.optimization_barrier((early, across, diagonal))
    tables = [early, best_of(across, diagonal, halves)]
    return merge(tables).reshape(rows, cols)


def solution(mesh):
    split = Mesh(mesh.devices.reshape(4, 2, 8, 8), ("sx",) + COLS)
    return jax.shard_map(
        on_device,
        mesh=split,
        in_specs=(
            P("sx", COLS, None),
            P(None, "sx", COLS),
            P(None, COLS),
        ),
        out_specs=P("sx", COLS),
        check_vma=False,
    )
```

```python
import jax
import jax.numpy as jnp
from jax import lax
from jax.experimental import pallas as pl
from jax.experimental.pallas import tpu as pltpu
from jax.sharding import Mesh
from jax.sharding import PartitionSpec as P

PH = 40
PW = 40
PIX = PH * PW
WIDE = 1792
COLS = ("sy", "z", "y")


def average_kernel(block_ref, far_ref, near_ref, weight_ref, out_ref):
    f32 = jnp.float32
    even = weight_ref[0, 0:1, 10:11] > 0.0
    lines = []
    for row in range(4):
        far, near = far_ref[row].astype(f32), near_ref[row].astype(f32)
        sides = jnp.where(even, far, near), jnp.where(even, near, far)
        lines.append(jnp.concatenate([sides[0], block_ref[row].astype(f32), sides[1]], axis=0))
    averaged = []
    for row in range(2):
        weight = weight_ref[row]
        total = jnp.zeros((4, PIX), f32)
        for row_step in range(3):
            for col_step in range(3):
                index = 3 * row_step + col_step
                near = lines[row + row_step][col_step : col_step + 4]
                total = total + weight[:, index : index + 1] * near
        averaged.append(total / weight[:, 9:10])
    image = jnp.concatenate(averaged, axis=0)
    image = jnp.concatenate([image, jnp.zeros((8, WIDE - PIX), f32)], axis=1)
    pixel = lax.broadcasted_iota(jnp.int32, (8, WIDE), 1)
    column = pixel % PW
    vertical = image
    for offset in (-2, -1, 1, 2):
        vertical = vertical + pltpu.roll(image, (-offset * PW) % WIDE, 1)
    box = vertical
    for offset in (-2, -1, 1, 2):
        inside = (column + offset >= 0) & (column + offset < PW)
        box = box + jnp.where(inside, pltpu.roll(vertical, (-offset) % WIDE, 1), 0.0)
    high = jnp.where(pixel < PIX, image - box / 25.0, 0.0)
    mean = jnp.sum(high, axis=1, keepdims=True) / PIX
    centered = jnp.where(pixel < PIX, high - mean, 0.0)
    scale = jnp.sqrt(jnp.sum(centered * centered, axis=1, keepdims=True) / PIX + 1e-06)
    out_ref[...] = (centered / scale)[:, :PIX].astype(jnp.bfloat16)


def average(block, far, near, weights):
    return pl.pallas_call(
        average_kernel,
        out_shape=jax.ShapeDtypeStruct((8, PIX), jnp.bfloat16),
        in_specs=[pl.BlockSpec(memory_space=pltpu.VMEM)] * 4,
        out_specs=pl.BlockSpec(memory_space=pltpu.VMEM),
        compiler_params=pltpu.CompilerParams(vmem_limit_bytes=16 * 1024 * 1024),
        cost_estimate=pl.CostEstimate(flops=1000000, bytes_accessed=200000, transcendentals=0),
    )(block, far, near, weights)


def hold_kernel(own_ref, partner_ref, own_held, partner_held, sems):
    copies = [
        pltpu.make_async_copy(own_ref, own_held, sems.at[0]),
        pltpu.make_async_copy(partner_ref, partner_held, sems.at[1]),
    ]
    for copy in copies:
        copy.start()
    for copy in copies:
        copy.wait()


def hold(own, partner):
    return pl.pallas_call(
        hold_kernel,
        out_shape=[pltpu.VMEM(half.shape, half.dtype) for half in (own, partner)],
        in_specs=[pl.BlockSpec(memory_space=space) for space in (pltpu.HBM, pl.ANY)],
        out_specs=[pl.BlockSpec(memory_space=pltpu.VMEM)] * 2,
        scratch_shapes=[pltpu.SemaphoreType.DMA((2,))],
        compiler_params=pltpu.CompilerParams(vmem_limit_bytes=16 * 1024 * 1024),
        cost_estimate=pl.CostEstimate(
            flops=0, bytes_accessed=2 * 4 * own.size, transcendentals=0
        ),
    )(pltpu.with_memory_space_constraint(own, pltpu.HBM), partner)


def row_best(points, half):
    scores = jnp.dot(points, half, preferred_element_type=jnp.float32)
    return jnp.max(scores, axis=1)


def best_of(first, second, halves):
    points = jnp.concatenate([first, second], axis=0)
    return jnp.maximum(*[row_best(points, half) for half in halves])


def largest_kernel(shares_ref, out_ref):
    best = jnp.max(shares_ref[...], axis=0, keepdims=True)
    out_ref[...] = jnp.concatenate([best[:, 0:4], best[:, 4:8]], axis=0)


def largest(shares):
    return pl.pallas_call(
        largest_kernel,
        out_shape=jax.ShapeDtypeStruct((2, 4), jnp.float32),
        in_specs=[pl.BlockSpec(memory_space=pltpu.VMEM)],
        out_specs=pl.BlockSpec(memory_space=pltpu.VMEM),
        cost_estimate=pl.CostEstimate(flops=512, bytes_accessed=4096, transcendentals=0),
    )(shares)


def place(core, z, y):
    return 64 * core + 8 * (z % 8) + y % 8


def parity_class(core, z_odd, y_odd):
    return [place(core, z, y) for z in range(z_odd, 8, 2) for y in range(y_odd, 8, 2)]


PARITIES = [(0, 0), (0, 1), (1, 0), (1, 1)]


def gather_class(block):
    groups = [parity_class(core, z, y) for core in range(2) for z, y in PARITIES]
    copies = jnp.broadcast_to(block[None], (16,) + block.shape)
    got = lax.all_to_all(copies, COLS, 0, 0, axis_index_groups=groups)
    return got.reshape(-1, block.shape[1])


def from_neighbour(block, z_step, y_step):
    pairs = []
    for core, sign in ((0, 1), (1, -1)):
        for z in range(8):
            for y in range(8):
                source = place(core, z + sign * z_step, y + sign * y_step)
                pairs.append((source, place(core, z, y)))
    return lax.ppermute(block, COLS, pairs)


def merge(tables):
    table = jnp.stack([pair.reshape(2, 128) for pair in tables])
    table = jnp.where(lax.axis_index("z") % 2 == 1, table[::-1], table)
    table = jnp.where(lax.axis_index("y") % 2 == 1, table[:, ::-1], table)
    groups = [sum([parity_class(core, z, y) for z, y in PARITIES], []) for core in range(2)]
    shares = lax.all_to_all(table.reshape(64, -1), COLS, 0, 0, axis_index_groups=groups)
    return largest(shares)


def swap_pairs(starts):
    return [pair for i in starts for pair in ((i, i + 1), (i + 1, i))]


def rim(patterns):
    odd = lax.axis_index("sx") % 2 == 1
    near = lax.ppermute(patterns, "sx", swap_pairs((0, 2)))
    far = lax.ppermute(patterns, "sx", swap_pairs((1,)))
    above = jnp.where(odd, near[1:], far[1:])
    below = jnp.where(odd, far[:1], near[:1])
    block = jnp.concatenate([above, patterns, below], axis=0)
    even = lax.axis_index(COLS) % 2 == 0
    first, last = block[:, 0:1], block[:, 3:4]
    far = lax.ppermute(jnp.where(even, first, last), COLS, swap_pairs(range(1, 127, 2)))
    near = lax.ppermute(jnp.where(even, last, first), COLS, swap_pairs(range(0, 128, 2)))
    return block, far, near


def valid_weights(weights, rows, cols):
    row = lax.axis_index("sx") * rows + jnp.arange(rows)
    col = lax.axis_index(COLS) * cols + jnp.arange(cols)
    steps = jnp.arange(-1, 2)
    row_near = row[:, None] + steps
    col_near = col[:, None] + steps
    row_valid = (row_near >= 0) & (row_near < rows * lax.axis_size("sx"))
    col_valid = (col_near >= 0) & (col_near < cols * lax.axis_size(COLS))
    valid = row_valid[:, None, :, None] & col_valid[None, :, None, :]
    kept = jnp.where(valid.reshape(rows, cols, 9), jnp.transpose(weights, (1, 2, 0)), 0.0)
    total = jnp.sum(kept, axis=2, keepdims=True)
    even = (lax.axis_index(COLS) % 2 == 0).astype(jnp.float32)
    return jnp.concatenate([kept, total, jnp.full_like(total, even)], axis=2)


def on_device(patterns, nlpar_weights, dictionary):
    rows, cols = patterns.shape[:2]
    shared, patterns = lax.optimization_barrier((dictionary, patterns))
    partner = lax.ppermute(shared, "sy", [(0, 1), (1, 0)])
    weights = valid_weights(nlpar_weights, rows, cols)
    normalized = average(*rim(patterns), weights)
    own = gather_class(normalized)
    ahead = from_neighbour(own, 0, 1)
    across = from_neighbour(own, 1, 0)
    diagonal = from_neighbour(own, 1, 1)
    own, *halves = lax.optimization_barrier((own, dictionary, partner))
    halves = hold(*halves)
    early = best_of(own, ahead, halves)
    early, across, diagonal = lax.optimization_barrier((early, across, diagonal))
    tables = [early, best_of(across, diagonal, halves)]
    return merge(tables)


def solution(mesh):
    split = Mesh(mesh.devices.reshape(4, 2, 8, 8), ("sx",) + COLS)
    return jax.shard_map(
        on_device,
        mesh=split,
        in_specs=(
            P("sx", COLS, None),
            P(None, "sx", COLS),
            P(None, COLS),
        ),
        out_specs=P("sx", COLS),
        check_vma=False,
    )
```

```python
import jax
import jax.numpy as jnp
from jax import lax
from jax.experimental import pallas as pl
from jax.experimental.pallas import tpu as pltpu
from jax.sharding import Mesh
from jax.sharding import PartitionSpec as P

PH = 40
PW = 40
PIX = PH * PW
WIDE = 1792
COLS = ("sy", "z", "y")


def average_kernel(block_ref, far_ref, near_ref, weight_ref, out_ref):
    f32 = jnp.float32
    even = weight_ref[0, 0:1, 10:11] > 0.0
    lines = []
    for row in range(4):
        far, near = far_ref[row].astype(f32), near_ref[row].astype(f32)
        sides = jnp.where(even, far, near), jnp.where(even, near, far)
        lines.append(jnp.concatenate([sides[0], block_ref[row].astype(f32), sides[1]], axis=0))
    averaged = []
    for row in range(2):
        weight = weight_ref[row]
        total = jnp.zeros((4, PIX), f32)
        for row_step in range(3):
            for col_step in range(3):
                index = 3 * row_step + col_step
                near = lines[row + row_step][col_step : col_step + 4]
                total = total + weight[:, index : index + 1] * near
        averaged.append(total / weight[:, 9:10])
    image = jnp.concatenate(averaged, axis=0)
    image = jnp.concatenate([image, jnp.zeros((8, WIDE - PIX), f32)], axis=1)
    pixel = lax.broadcasted_iota(jnp.int32, (8, WIDE), 1)
    column = pixel % PW
    vertical = image
    for offset in (-2, -1, 1, 2):
        vertical = vertical + pltpu.roll(image, (-offset * PW) % WIDE, 1)
    box = vertical
    for offset in (-2, -1, 1, 2):
        inside = (column + offset >= 0) & (column + offset < PW)
        box = box + jnp.where(inside, pltpu.roll(vertical, (-offset) % WIDE, 1), 0.0)
    high = jnp.where(pixel < PIX, image - box / 25.0, 0.0)
    mean = jnp.sum(high, axis=1, keepdims=True) / PIX
    centered = jnp.where(pixel < PIX, high - mean, 0.0)
    scale = jnp.sqrt(jnp.sum(centered * centered, axis=1, keepdims=True) / PIX + 1e-06)
    out_ref[...] = (centered / scale)[:, :PIX].astype(jnp.bfloat16)


def average(block, far, near, weights):
    return pl.pallas_call(
        average_kernel,
        out_shape=jax.ShapeDtypeStruct((8, PIX), jnp.bfloat16),
        in_specs=[pl.BlockSpec(memory_space=pltpu.VMEM)] * 4,
        out_specs=pl.BlockSpec(memory_space=pltpu.VMEM),
        compiler_params=pltpu.CompilerParams(vmem_limit_bytes=16 * 1024 * 1024),
        cost_estimate=pl.CostEstimate(flops=1000000, bytes_accessed=200000, transcendentals=0),
    )(block, far, near, weights)


def hold_kernel(own_ref, partner_ref, own_held, partner_held, sems):
    copies = [
        pltpu.make_async_copy(own_ref, own_held, sems.at[0]),
        pltpu.make_async_copy(partner_ref, partner_held, sems.at[1]),
    ]
    for copy in copies:
        copy.start()
    for copy in copies:
        copy.wait()


def hold(own, partner):
    return pl.pallas_call(
        hold_kernel,
        out_shape=[pltpu.VMEM(half.shape, half.dtype) for half in (own, partner)],
        in_specs=[pl.BlockSpec(memory_space=space) for space in (pltpu.HBM, pl.ANY)],
        out_specs=[pl.BlockSpec(memory_space=pltpu.VMEM)] * 2,
        scratch_shapes=[pltpu.SemaphoreType.DMA((2,))],
        compiler_params=pltpu.CompilerParams(vmem_limit_bytes=16 * 1024 * 1024),
        cost_estimate=pl.CostEstimate(
            flops=0, bytes_accessed=2 * 4 * own.size, transcendentals=0
        ),
    )(pltpu.with_memory_space_constraint(own, pltpu.HBM), partner)


def row_best(points, half):
    scores = jnp.dot(points, half, preferred_element_type=jnp.float32)
    return jnp.max(scores, axis=1)


def best_of(first, second, halves):
    points = jnp.concatenate([first, second], axis=0)
    return jnp.maximum(*[row_best(points, half) for half in halves])


def place(core, z, y):
    return 64 * core + 8 * (z % 8) + y % 8


def parity_class(core, z_odd, y_odd):
    return [place(core, z, y) for z in range(z_odd, 8, 2) for y in range(y_odd, 8, 2)]


PARITIES = [(0, 0), (0, 1), (1, 0), (1, 1)]


def gather_class(block):
    groups = [parity_class(core, z, y) for core in range(2) for z, y in PARITIES]
    copies = jnp.broadcast_to(block[None], (16,) + block.shape)
    got = lax.all_to_all(copies, COLS, 0, 0, axis_index_groups=groups)
    return got.reshape(-1, block.shape[1])


def from_neighbour(block, z_step, y_step):
    pairs = []
    for core, sign in ((0, 1), (1, -1)):
        for z in range(8):
            for y in range(8):
                source = place(core, z + sign * z_step, y + sign * y_step)
                pairs.append((source, place(core, z, y)))
    return lax.ppermute(block, COLS, pairs)


def merge(tables):
    table = jnp.stack([pair.reshape(2, 128) for pair in tables])
    table = jnp.where(lax.axis_index("z") % 2 == 1, table[::-1], table)
    table = jnp.where(lax.axis_index("y") % 2 == 1, table[:, ::-1], table)
    table = jnp.transpose(table.reshape(2, 2, 4, 4, 8), (2, 0, 3, 1, 4)).reshape(64, 8)
    groups = [[place(core, z, y) for z in range(8) for y in range(8)] for core in range(2)]
    shares = lax.all_to_all(table, COLS, 0, 0, axis_index_groups=groups)
    return jnp.max(shares, axis=0)


def swap_pairs(starts):
    return [pair for i in starts for pair in ((i, i + 1), (i + 1, i))]


def rim(patterns):
    odd = lax.axis_index("sx") % 2 == 1
    near = lax.ppermute(patterns, "sx", swap_pairs((0, 2)))
    far = lax.ppermute(patterns, "sx", swap_pairs((1,)))
    above = jnp.where(odd, near[1:], far[1:])
    below = jnp.where(odd, far[:1], near[:1])
    block = jnp.concatenate([above, patterns, below], axis=0)
    even = lax.axis_index(COLS) % 2 == 0
    first, last = block[:, 0:1], block[:, 3:4]
    far = lax.ppermute(jnp.where(even, first, last), COLS, swap_pairs(range(1, 127, 2)))
    near = lax.ppermute(jnp.where(even, last, first), COLS, swap_pairs(range(0, 128, 2)))
    return block, far, near


def valid_weights(weights, rows, cols):
    row = lax.axis_index("sx") * rows + jnp.arange(rows)
    col = lax.axis_index(COLS) * cols + jnp.arange(cols)
    steps = jnp.arange(-1, 2)
    row_near = row[:, None] + steps
    col_near = col[:, None] + steps
    row_valid = (row_near >= 0) & (row_near < rows * lax.axis_size("sx"))
    col_valid = (col_near >= 0) & (col_near < cols * lax.axis_size(COLS))
    valid = row_valid[:, None, :, None] & col_valid[None, :, None, :]
    kept = jnp.where(valid.reshape(rows, cols, 9), jnp.transpose(weights, (1, 2, 0)), 0.0)
    total = jnp.sum(kept, axis=2, keepdims=True)
    even = (lax.axis_index(COLS) % 2 == 0).astype(jnp.float32)
    return jnp.concatenate([kept, total, jnp.full_like(total, even)], axis=2)


def on_device(patterns, nlpar_weights, dictionary):
    rows, cols = patterns.shape[:2]
    shared, patterns = lax.optimization_barrier((dictionary, patterns))
    partner = lax.ppermute(shared, "sy", [(0, 1), (1, 0)])
    weights = valid_weights(nlpar_weights, rows, cols)
    normalized = average(*rim(patterns), weights)
    own = gather_class(normalized)
    ahead = from_neighbour(own, 0, 1)
    across = from_neighbour(own, 1, 0)
    diagonal = from_neighbour(own, 1, 1)
    own, *halves = lax.optimization_barrier((own, dictionary, partner))
    halves = hold(*halves)
    early = best_of(own, ahead, halves)
    early, across, diagonal = lax.optimization_barrier((early, across, diagonal))
    tables = [early, best_of(across, diagonal, halves)]
    return merge(tables).reshape(rows, cols)


def solution(mesh):
    split = Mesh(mesh.devices.reshape(4, 2, 8, 8), ("sx",) + COLS)
    return jax.shard_map(
        on_device,
        mesh=split,
        in_specs=(
            P("sx", COLS, None),
            P(None, "sx", COLS),
            P(None, COLS),
        ),
        out_specs=P("sx", COLS),
        check_vma=False,
    )
```

```python
import jax
import jax.numpy as jnp
from jax import lax
from jax.experimental import pallas as pl
from jax.experimental.pallas import tpu as pltpu
from jax.sharding import Mesh
from jax.sharding import PartitionSpec as P

PH = 40
PW = 40
PIX = PH * PW
WIDE = 1792
COLS = ("sy", "z", "y")


def average_kernel(block_ref, far_ref, near_ref, weight_ref, out_ref):
    f32 = jnp.float32
    even = weight_ref[0, 0:1, 10:11] > 0.0
    lines = []
    for row in range(4):
        far, near = far_ref[row].astype(f32), near_ref[row].astype(f32)
        sides = jnp.where(even, far, near), jnp.where(even, near, far)
        lines.append(jnp.concatenate([sides[0], block_ref[row].astype(f32), sides[1]], axis=0))
    averaged = []
    for row in range(2):
        weight = weight_ref[row]
        total = jnp.zeros((4, PIX), f32)
        for row_step in range(3):
            for col_step in range(3):
                index = 3 * row_step + col_step
                near = lines[row + row_step][col_step : col_step + 4]
                total = total + weight[:, index : index + 1] * near
        averaged.append(total / weight[:, 9:10])
    image = jnp.concatenate(averaged, axis=0)
    image = jnp.concatenate([image, jnp.zeros((8, WIDE - PIX), f32)], axis=1)
    pixel = lax.broadcasted_iota(jnp.int32, (8, WIDE), 1)
    column = pixel % PW
    vertical = image
    for offset in (-2, -1, 1, 2):
        vertical = vertical + pltpu.roll(image, (-offset * PW) % WIDE, 1)
    box = vertical
    for offset in (-2, -1, 1, 2):
        inside = (column + offset >= 0) & (column + offset < PW)
        box = box + jnp.where(inside, pltpu.roll(vertical, (-offset) % WIDE, 1), 0.0)
    high = jnp.where(pixel < PIX, image - box / 25.0, 0.0)
    mean = jnp.sum(high, axis=1, keepdims=True) / PIX
    centered = jnp.where(pixel < PIX, high - mean, 0.0)
    scale = jnp.sqrt(jnp.sum(centered * centered, axis=1, keepdims=True) / PIX + 1e-06)
    out_ref[...] = (centered / scale)[:, :PIX].astype(jnp.bfloat16)


def average(block, far, near, weights):
    return pl.pallas_call(
        average_kernel,
        out_shape=jax.ShapeDtypeStruct((8, PIX), jnp.bfloat16),
        in_specs=[pl.BlockSpec(memory_space=pltpu.VMEM)] * 4,
        out_specs=pl.BlockSpec(memory_space=pltpu.VMEM),
        compiler_params=pltpu.CompilerParams(vmem_limit_bytes=16 * 1024 * 1024),
        cost_estimate=pl.CostEstimate(flops=1000000, bytes_accessed=200000, transcendentals=0),
    )(block, far, near, weights)


def hold_kernel(own_ref, partner_ref, own_held, partner_held, sems):
    copies = [
        pltpu.make_async_copy(own_ref, own_held, sems.at[0]),
        pltpu.make_async_copy(partner_ref, partner_held, sems.at[1]),
    ]
    for copy in copies:
        copy.start()
    for copy in copies:
        copy.wait()


def hold(own, partner):
    return pl.pallas_call(
        hold_kernel,
        out_shape=[pltpu.VMEM(half.shape, half.dtype) for half in (own, partner)],
        in_specs=[pl.BlockSpec(memory_space=space) for space in (pltpu.HBM, pl.ANY)],
        out_specs=[pl.BlockSpec(memory_space=pltpu.VMEM)] * 2,
        scratch_shapes=[pltpu.SemaphoreType.DMA((2,))],
        compiler_params=pltpu.CompilerParams(vmem_limit_bytes=16 * 1024 * 1024),
        cost_estimate=pl.CostEstimate(
            flops=0, bytes_accessed=2 * 4 * own.size, transcendentals=0
        ),
    )(pltpu.with_memory_space_constraint(own, pltpu.HBM), partner)


def row_best(points, half):
    scores = jnp.dot(points, half, preferred_element_type=jnp.float32)
    return jnp.max(scores, axis=1)


def best_of(first, second, halves):
    points = jnp.concatenate([first, second], axis=0)
    return jnp.maximum(*[row_best(points, half) for half in halves])


def place(core, z, y):
    return 64 * core + 8 * (z % 8) + y % 8


def parity_class(core, z_odd, y_odd):
    return [place(core, z, y) for z in range(z_odd, 8, 2) for y in range(y_odd, 8, 2)]


PARITIES = [(0, 0), (0, 1), (1, 0), (1, 1)]


def gather_class(block):
    groups = [parity_class(core, z, y) for core in range(2) for z, y in PARITIES]
    copies = jnp.broadcast_to(block[None], (16,) + block.shape)
    got = lax.all_to_all(copies, COLS, 0, 0, axis_index_groups=groups)
    return got.reshape(-1, block.shape[1])


def from_neighbour(block, z_step, y_step):
    pairs = []
    for core, sign in ((0, 1), (1, -1)):
        for z in range(8):
            for y in range(8):
                source = place(core, z + sign * z_step, y + sign * y_step)
                pairs.append((source, place(core, z, y)))
    return lax.ppermute(block, COLS, pairs)


def merge(tables):
    table = jnp.stack([pair.reshape(2, 128) for pair in tables])
    table = jnp.where(lax.axis_index("z") % 2 == 1, table[::-1], table)
    table = jnp.where(lax.axis_index("y") % 2 == 1, table[:, ::-1], table)
    table = jnp.transpose(table.reshape(2, 2, 4, 4, 8), (2, 0, 3, 1, 4)).reshape(64, 8)
    groups = [[place(core, z, y) for z in range(8) for y in range(8)] for core in range(2)]
    shares = lax.all_to_all(table, COLS, 0, 0, axis_index_groups=groups)
    return jnp.max(shares, axis=0)


def swap_pairs(starts):
    return [pair for i in starts for pair in ((i, i + 1), (i + 1, i))]


def rim(patterns):
    plane = lax.axis_index("sx")
    ahead = (jnp.arange(4) > plane)[:, None, None]
    rows = lax.all_to_all(jnp.where(ahead, patterns[1], patterns[0]), "sx", 0, 0)
    above = lax.dynamic_slice_in_dim(rows, jnp.maximum(plane - 1, 0), 1, 0)
    below = lax.dynamic_slice_in_dim(rows, jnp.minimum(plane + 1, 3), 1, 0)
    block = jnp.concatenate([above, patterns, below], axis=0)
    even = lax.axis_index(COLS) % 2 == 0
    first, last = block[:, 0:1], block[:, 3:4]
    far = lax.ppermute(jnp.where(even, first, last), COLS, swap_pairs(range(1, 127, 2)))
    near = lax.ppermute(jnp.where(even, last, first), COLS, swap_pairs(range(0, 128, 2)))
    return block, far, near


def valid_weights(weights, rows, cols):
    row = lax.axis_index("sx") * rows + jnp.arange(rows)
    col = lax.axis_index(COLS) * cols + jnp.arange(cols)
    steps = jnp.arange(-1, 2)
    row_near = row[:, None] + steps
    col_near = col[:, None] + steps
    row_valid = (row_near >= 0) & (row_near < rows * lax.axis_size("sx"))
    col_valid = (col_near >= 0) & (col_near < cols * lax.axis_size(COLS))
    valid = row_valid[:, None, :, None] & col_valid[None, :, None, :]
    kept = jnp.where(valid.reshape(rows, cols, 9), jnp.transpose(weights, (1, 2, 0)), 0.0)
    total = jnp.sum(kept, axis=2, keepdims=True)
    even = (lax.axis_index(COLS) % 2 == 0).astype(jnp.float32)
    return jnp.concatenate([kept, total, jnp.full_like(total, even)], axis=2)


def on_device(patterns, nlpar_weights, dictionary):
    rows, cols = patterns.shape[:2]
    shared, patterns = lax.optimization_barrier((dictionary, patterns))
    partner = lax.ppermute(shared, "sy", [(0, 1), (1, 0)])
    weights = valid_weights(nlpar_weights, rows, cols)
    normalized = average(*rim(patterns), weights)
    own = gather_class(normalized)
    ahead = from_neighbour(own, 0, 1)
    across = from_neighbour(own, 1, 0)
    diagonal = from_neighbour(own, 1, 1)
    own, *halves = lax.optimization_barrier((own, dictionary, partner))
    halves = hold(*halves)
    early = best_of(own, ahead, halves)
    early, across, diagonal = lax.optimization_barrier((early, across, diagonal))
    tables = [early, best_of(across, diagonal, halves)]
    return merge(tables).reshape(rows, cols)


def solution(mesh):
    split = Mesh(mesh.devices.reshape(4, 2, 8, 8), ("sx",) + COLS)
    return jax.shard_map(
        on_device,
        mesh=split,
        in_specs=(
            P("sx", COLS, None),
            P(None, "sx", COLS),
            P(None, COLS),
        ),
        out_specs=P("sx", COLS),
        check_vma=False,
    )
```

```python
import jax
import jax.numpy as jnp
from jax import lax
from jax.experimental import pallas as pl
from jax.experimental.pallas import tpu as pltpu
from jax.sharding import Mesh
from jax.sharding import PartitionSpec as P

PH = 40
PW = 40
PIX = PH * PW
WIDE = 1792
SPLIT = ("sx", "sy", "z_pair", "z_odd", "y_pair", "y_odd")
COLS = SPLIT[1:]


def average_kernel(block_ref, far_ref, near_ref, weight_ref, out_ref):
    f32 = jnp.float32
    even = weight_ref[0, 0:1, 10:11] > 0.0
    lines = []
    for row in range(4):
        far, near = far_ref[row].astype(f32), near_ref[row].astype(f32)
        sides = jnp.where(even, far, near), jnp.where(even, near, far)
        lines.append(jnp.concatenate([sides[0], block_ref[row].astype(f32), sides[1]], axis=0))
    averaged = []
    for row in range(2):
        weight = weight_ref[row]
        total = jnp.zeros((4, PIX), f32)
        for row_step in range(3):
            for col_step in range(3):
                index = 3 * row_step + col_step
                near = lines[row + row_step][col_step : col_step + 4]
                total = total + weight[:, index : index + 1] * near
        averaged.append(total / weight[:, 9:10])
    image = jnp.concatenate(averaged, axis=0)
    image = jnp.concatenate([image, jnp.zeros((8, WIDE - PIX), f32)], axis=1)
    pixel = lax.broadcasted_iota(jnp.int32, (8, WIDE), 1)
    column = pixel % PW
    vertical = image
    for offset in (-2, -1, 1, 2):
        vertical = vertical + pltpu.roll(image, (-offset * PW) % WIDE, 1)
    box = vertical
    for offset in (-2, -1, 1, 2):
        inside = (column + offset >= 0) & (column + offset < PW)
        box = box + jnp.where(inside, pltpu.roll(vertical, (-offset) % WIDE, 1), 0.0)
    high = jnp.where(pixel < PIX, image - box / 25.0, 0.0)
    mean = jnp.sum(high, axis=1, keepdims=True) / PIX
    centered = jnp.where(pixel < PIX, high - mean, 0.0)
    scale = jnp.sqrt(jnp.sum(centered * centered, axis=1, keepdims=True) / PIX + 1e-06)
    out_ref[...] = (centered / scale)[:, :PIX].astype(jnp.bfloat16)


def average(block, far, near, weights):
    return pl.pallas_call(
        average_kernel,
        out_shape=jax.ShapeDtypeStruct((8, PIX), jnp.bfloat16),
        in_specs=[pl.BlockSpec(memory_space=pltpu.VMEM)] * 4,
        out_specs=pl.BlockSpec(memory_space=pltpu.VMEM),
        compiler_params=pltpu.CompilerParams(vmem_limit_bytes=16 * 1024 * 1024),
        cost_estimate=pl.CostEstimate(flops=1000000, bytes_accessed=200000, transcendentals=0),
    )(block, far, near, weights)


def hold_kernel(own_ref, partner_ref, own_held, partner_held, sems):
    copies = [
        pltpu.make_async_copy(own_ref, own_held, sems.at[0]),
        pltpu.make_async_copy(partner_ref, partner_held, sems.at[1]),
    ]
    for copy in copies:
        copy.start()
    for copy in copies:
        copy.wait()


def hold(own, partner):
    return pl.pallas_call(
        hold_kernel,
        out_shape=[pltpu.VMEM(half.shape, half.dtype) for half in (own, partner)],
        in_specs=[pl.BlockSpec(memory_space=space) for space in (pltpu.HBM, pl.ANY)],
        out_specs=[pl.BlockSpec(memory_space=pltpu.VMEM)] * 2,
        scratch_shapes=[pltpu.SemaphoreType.DMA((2,))],
        compiler_params=pltpu.CompilerParams(vmem_limit_bytes=16 * 1024 * 1024),
        cost_estimate=pl.CostEstimate(
            flops=0, bytes_accessed=2 * 4 * own.size, transcendentals=0
        ),
    )(pltpu.with_memory_space_constraint(own, pltpu.HBM), partner)


def row_best(points, half):
    scores = jnp.dot(points, half, preferred_element_type=jnp.float32)
    return jnp.max(scores, axis=1)


def best_of(first, second, halves):
    points = jnp.concatenate([first, second], axis=0)
    return jnp.maximum(*[row_best(points, half) for half in halves])


def place(core, z, y):
    return 64 * core + 8 * (z % 8) + y % 8


def gather_class(block):
    copies = jnp.broadcast_to(block[None], (16,) + block.shape)
    got = lax.all_to_all(copies, ("z_pair", "y_pair"), 0, 0)
    return got.reshape(-1, block.shape[1])


def from_neighbour(block, z_step, y_step):
    pairs = []
    for core, sign in ((0, 1), (1, -1)):
        for z in range(8):
            for y in range(8):
                source = place(core, z + sign * z_step, y + sign * y_step)
                pairs.append((source, place(core, z, y)))
    return lax.ppermute(block, COLS, pairs)


def merge(tables):
    table = jnp.stack([pair.reshape(2, 128) for pair in tables])
    table = jnp.where(lax.axis_index("z_odd") == 1, table[::-1], table)
    table = jnp.where(lax.axis_index("y_odd") == 1, table[:, ::-1], table)
    table = jnp.transpose(table.reshape(2, 2, 4, 4, 8), (2, 0, 3, 1, 4)).reshape(64, 8)
    shares = lax.all_to_all(table, COLS[1:], 0, 0)
    return jnp.max(shares, axis=0)


def swap_pairs(starts):
    return [pair for i in starts for pair in ((i, i + 1), (i + 1, i))]


def rim(patterns):
    odd = lax.axis_index("sx") % 2 == 1
    near = lax.ppermute(patterns, "sx", swap_pairs((0, 2)))
    far = lax.ppermute(patterns, "sx", swap_pairs((1,)))
    above = jnp.where(odd, near[1:], far[1:])
    below = jnp.where(odd, far[:1], near[:1])
    block = jnp.concatenate([above, patterns, below], axis=0)
    even = lax.axis_index(COLS) % 2 == 0
    first, last = block[:, 0:1], block[:, 3:4]
    far = lax.ppermute(jnp.where(even, first, last), COLS, swap_pairs(range(1, 127, 2)))
    near = lax.ppermute(jnp.where(even, last, first), COLS, swap_pairs(range(0, 128, 2)))
    return block, far, near


def valid_weights(weights, rows, cols):
    row = lax.axis_index("sx") * rows + jnp.arange(rows)
    col = lax.axis_index(COLS) * cols + jnp.arange(cols)
    steps = jnp.arange(-1, 2)
    row_near = row[:, None] + steps
    col_near = col[:, None] + steps
    row_valid = (row_near >= 0) & (row_near < rows * lax.axis_size("sx"))
    col_valid = (col_near >= 0) & (col_near < cols * lax.axis_size(COLS))
    valid = row_valid[:, None, :, None] & col_valid[None, :, None, :]
    kept = jnp.where(valid.reshape(rows, cols, 9), jnp.transpose(weights, (1, 2, 0)), 0.0)
    total = jnp.sum(kept, axis=2, keepdims=True)
    even = (lax.axis_index(COLS) % 2 == 0).astype(jnp.float32)
    return jnp.concatenate([kept, total, jnp.full_like(total, even)], axis=2)


def on_device(patterns, nlpar_weights, dictionary):
    rows, cols = patterns.shape[:2]
    shared, patterns = lax.optimization_barrier((dictionary, patterns))
    partner = lax.ppermute(shared, "sy", [(0, 1), (1, 0)])
    weights = valid_weights(nlpar_weights, rows, cols)
    normalized = average(*rim(patterns), weights)
    own = gather_class(normalized)
    ahead = from_neighbour(own, 0, 1)
    across = from_neighbour(own, 1, 0)
    diagonal = from_neighbour(own, 1, 1)
    own, *halves = lax.optimization_barrier((own, dictionary, partner))
    halves = hold(*halves)
    early = best_of(own, ahead, halves)
    early, across, diagonal = lax.optimization_barrier((early, across, diagonal))
    tables = [early, best_of(across, diagonal, halves)]
    return merge(tables).reshape(rows, cols)


def solution(mesh):
    split = Mesh(mesh.devices.reshape(4, 2, 4, 2, 4, 2), SPLIT)
    return jax.shard_map(
        on_device,
        mesh=split,
        in_specs=(
            P("sx", COLS, None),
            P(None, "sx", COLS),
            P(None, COLS),
        ),
        out_specs=P("sx", COLS),
        check_vma=False,
    )
```

```python
import jax
import jax.numpy as jnp
from jax import lax
from jax.experimental import pallas as pl
from jax.experimental.pallas import tpu as pltpu
from jax.sharding import Mesh
from jax.sharding import PartitionSpec as P

PH = 40
PW = 40
PIX = PH * PW
WIDE = 1792
COLS = ("sy", "z", "y")


def average_kernel(block_ref, far_ref, near_ref, weight_ref, out_ref):
    f32 = jnp.float32
    even = weight_ref[0, 0:1, 10:11] > 0.0
    lines = []
    for row in range(4):
        far, near = far_ref[row].astype(f32), near_ref[row].astype(f32)
        sides = jnp.where(even, far, near), jnp.where(even, near, far)
        lines.append(jnp.concatenate([sides[0], block_ref[row].astype(f32), sides[1]], axis=0))
    averaged = []
    for row in range(2):
        weight = weight_ref[row]
        total = jnp.zeros((4, PIX), f32)
        for row_step in range(3):
            for col_step in range(3):
                index = 3 * row_step + col_step
                near = lines[row + row_step][col_step : col_step + 4]
                total = total + weight[:, index : index + 1] * near
        averaged.append(total / weight[:, 9:10])
    image = jnp.concatenate(averaged, axis=0)
    image = jnp.concatenate([image, jnp.zeros((8, WIDE - PIX), f32)], axis=1)
    pixel = lax.broadcasted_iota(jnp.int32, (8, WIDE), 1)
    column = pixel % PW
    vertical = image
    for offset in (-2, -1, 1, 2):
        vertical = vertical + pltpu.roll(image, (-offset * PW) % WIDE, 1)
    box = vertical
    for offset in (-2, -1, 1, 2):
        inside = (column + offset >= 0) & (column + offset < PW)
        box = box + jnp.where(inside, pltpu.roll(vertical, (-offset) % WIDE, 1), 0.0)
    high = jnp.where(pixel < PIX, image - box / 25.0, 0.0)
    mean = jnp.sum(high, axis=1, keepdims=True) / PIX
    centered = jnp.where(pixel < PIX, high - mean, 0.0)
    scale = jnp.sqrt(jnp.sum(centered * centered, axis=1, keepdims=True) / PIX + 1e-06)
    out_ref[...] = (centered / scale)[:, :PIX].astype(jnp.bfloat16)


def average(block, far, near, weights):
    return pl.pallas_call(
        average_kernel,
        out_shape=jax.ShapeDtypeStruct((8, PIX), jnp.bfloat16),
        in_specs=[pl.BlockSpec(memory_space=pltpu.VMEM)] * 4,
        out_specs=pl.BlockSpec(memory_space=pltpu.VMEM),
        compiler_params=pltpu.CompilerParams(vmem_limit_bytes=16 * 1024 * 1024),
        cost_estimate=pl.CostEstimate(flops=1000000, bytes_accessed=200000, transcendentals=0),
    )(block, far, near, weights)


def hold_kernel(own_ref, partner_ref, held_ref, sems):
    columns = own_ref.shape[1]
    copies = [
        pltpu.make_async_copy(own_ref, held_ref.at[:, pl.ds(0, columns)], sems.at[0]),
        pltpu.make_async_copy(partner_ref, held_ref.at[:, pl.ds(columns, columns)], sems.at[1]),
    ]
    for copy in copies:
        copy.start()
    for copy in copies:
        copy.wait()


def hold(own, partner):
    return pl.pallas_call(
        hold_kernel,
        out_shape=pltpu.VMEM((own.shape[0], 2 * own.shape[1]), own.dtype),
        in_specs=[pl.BlockSpec(memory_space=space) for space in (pltpu.HBM, pl.ANY)],
        out_specs=pl.BlockSpec(memory_space=pltpu.VMEM),
        scratch_shapes=[pltpu.SemaphoreType.DMA((2,))],
        compiler_params=pltpu.CompilerParams(vmem_limit_bytes=16 * 1024 * 1024),
        cost_estimate=pl.CostEstimate(
            flops=0, bytes_accessed=2 * 4 * own.size, transcendentals=0
        ),
    )(pltpu.with_memory_space_constraint(own, pltpu.HBM), partner)


def best_of(first, second, held):
    points = jnp.concatenate([first, second], axis=0)
    return jnp.max(jnp.dot(points, held, preferred_element_type=jnp.float32), axis=1)


def place(core, z, y):
    return 64 * core + 8 * (z % 8) + y % 8


def parity_class(core, z_odd, y_odd):
    return [place(core, z, y) for z in range(z_odd, 8, 2) for y in range(y_odd, 8, 2)]


PARITIES = [(0, 0), (0, 1), (1, 0), (1, 1)]


def gather_class(block):
    groups = [parity_class(core, z, y) for core in range(2) for z, y in PARITIES]
    copies = jnp.broadcast_to(block[None], (16,) + block.shape)
    got = lax.all_to_all(copies, COLS, 0, 0, axis_index_groups=groups)
    return got.reshape(-1, block.shape[1])


def from_neighbour(block, z_step, y_step):
    pairs = []
    for core, sign in ((0, 1), (1, -1)):
        for z in range(8):
            for y in range(8):
                source = place(core, z + sign * z_step, y + sign * y_step)
                pairs.append((source, place(core, z, y)))
    return lax.ppermute(block, COLS, pairs)


def merge(tables):
    table = jnp.stack([pair.reshape(2, 128) for pair in tables])
    table = jnp.where(lax.axis_index("z") % 2 == 1, table[::-1], table)
    table = jnp.where(lax.axis_index("y") % 2 == 1, table[:, ::-1], table)
    table = jnp.transpose(table.reshape(2, 2, 4, 4, 2, 4), (2, 0, 3, 1, 4, 5))
    groups = [[place(core, z, y) for z in range(8) for y in range(8)] for core in range(2)]
    shares = lax.all_to_all(table.reshape(64, 2, 4), COLS, 0, 0, axis_index_groups=groups)
    return jnp.max(shares, axis=0)


def swap_pairs(starts):
    return [pair for i in starts for pair in ((i, i + 1), (i + 1, i))]


def rim(patterns):
    odd = lax.axis_index("sx") % 2 == 1
    near = lax.ppermute(patterns, "sx", swap_pairs((0, 2)))
    far = lax.ppermute(patterns, "sx", swap_pairs((1,)))
    above = jnp.where(odd, near[1:], far[1:])
    below = jnp.where(odd, far[:1], near[:1])
    block = jnp.concatenate([above, patterns, below], axis=0)
    even = lax.axis_index(COLS) % 2 == 0
    first, last = block[:, 0:1], block[:, 3:4]
    far = lax.ppermute(jnp.where(even, first, last), COLS, swap_pairs(range(1, 127, 2)))
    near = lax.ppermute(jnp.where(even, last, first), COLS, swap_pairs(range(0, 128, 2)))
    return block, far, near


def valid_weights(weights, rows, cols):
    row = lax.axis_index("sx") * rows + jnp.arange(rows)
    col = lax.axis_index(COLS) * cols + jnp.arange(cols)
    steps = jnp.arange(-1, 2)
    row_near = row[:, None] + steps
    col_near = col[:, None] + steps
    row_valid = (row_near >= 0) & (row_near < rows * lax.axis_size("sx"))
    col_valid = (col_near >= 0) & (col_near < cols * lax.axis_size(COLS))
    valid = row_valid[:, None, :, None] & col_valid[None, :, None, :]
    kept = jnp.where(valid.reshape(rows, cols, 9), jnp.transpose(weights, (1, 2, 0)), 0.0)
    total = jnp.sum(kept, axis=2, keepdims=True)
    even = (lax.axis_index(COLS) % 2 == 0).astype(jnp.float32)
    return jnp.concatenate([kept, total, jnp.full_like(total, even)], axis=2)


def on_device(patterns, nlpar_weights, dictionary):
    rows, cols = patterns.shape[:2]
    shared, patterns = lax.optimization_barrier((dictionary, patterns))
    partner = lax.ppermute(shared, "sy", [(0, 1), (1, 0)])
    weights = valid_weights(nlpar_weights, rows, cols)
    normalized = average(*rim(patterns), weights)
    own = gather_class(normalized)
    ahead = from_neighbour(own, 0, 1)
    across = from_neighbour(own, 1, 0)
    diagonal = from_neighbour(own, 1, 1)
    own, *halves = lax.optimization_barrier((own, dictionary, partner))
    held = hold(*halves)
    early = best_of(own, ahead, held)
    early, across, diagonal = lax.optimization_barrier((early, across, diagonal))
    tables = [early, best_of(across, diagonal, held)]
    return merge(tables)


def solution(mesh):
    split = Mesh(mesh.devices.reshape(4, 2, 8, 8), ("sx",) + COLS)
    return jax.shard_map(
        on_device,
        mesh=split,
        in_specs=(
            P("sx", COLS, None),
            P(None, "sx", COLS),
            P(None, COLS),
        ),
        out_specs=P("sx", COLS),
        check_vma=False,
    )
```

```python
import jax
import jax.numpy as jnp
from jax import lax
from jax.experimental import pallas as pl
from jax.experimental.pallas import tpu as pltpu
from jax.sharding import Mesh
from jax.sharding import PartitionSpec as P

PH = 40
PW = 40
PIX = PH * PW
WIDE = 1792
COLS = ("sy", "z", "y")


def average_kernel(block_ref, far_ref, near_ref, weight_ref, out_ref):
    f32 = jnp.float32
    even = weight_ref[0, 0:1, 10:11] > 0.0
    lines = []
    for row in range(4):
        far, near = far_ref[row].astype(f32), near_ref[row].astype(f32)
        sides = jnp.where(even, far, near), jnp.where(even, near, far)
        lines.append(jnp.concatenate([sides[0], block_ref[row].astype(f32), sides[1]], axis=0))
    averaged = []
    for row in range(2):
        weight = weight_ref[row]
        total = jnp.zeros((4, PIX), f32)
        for row_step in range(3):
            for col_step in range(3):
                index = 3 * row_step + col_step
                near = lines[row + row_step][col_step : col_step + 4]
                total = total + weight[:, index : index + 1] * near
        averaged.append(total / weight[:, 9:10])
    image = jnp.concatenate(averaged, axis=0)
    image = jnp.concatenate([image, jnp.zeros((8, WIDE - PIX), f32)], axis=1)
    pixel = lax.broadcasted_iota(jnp.int32, (8, WIDE), 1)
    column = pixel % PW
    vertical = image
    for offset in (-2, -1, 1, 2):
        vertical = vertical + pltpu.roll(image, (-offset * PW) % WIDE, 1)
    box = vertical
    for offset in (-2, -1, 1, 2):
        inside = (column + offset >= 0) & (column + offset < PW)
        box = box + jnp.where(inside, pltpu.roll(vertical, (-offset) % WIDE, 1), 0.0)
    high = jnp.where(pixel < PIX, image - box / 25.0, 0.0)
    mean = jnp.sum(high, axis=1, keepdims=True) / PIX
    centered = jnp.where(pixel < PIX, high - mean, 0.0)
    scale = jnp.sqrt(jnp.sum(centered * centered, axis=1, keepdims=True) / PIX + 1e-06)
    out_ref[...] = (centered / scale)[:, :PIX].astype(jnp.bfloat16)


def average(block, far, near, weights):
    return pl.pallas_call(
        average_kernel,
        out_shape=jax.ShapeDtypeStruct((8, PIX), jnp.bfloat16),
        in_specs=[pl.BlockSpec(memory_space=pltpu.VMEM)] * 4,
        out_specs=pl.BlockSpec(memory_space=pltpu.VMEM),
        compiler_params=pltpu.CompilerParams(vmem_limit_bytes=16 * 1024 * 1024),
        cost_estimate=pl.CostEstimate(
            flops=100000000000, bytes_accessed=200000, transcendentals=0
        ),
    )(block, far, near, weights)


def hold_kernel(own_ref, partner_ref, held_ref, sems):
    columns = own_ref.shape[1]
    copies = [
        pltpu.make_async_copy(own_ref, held_ref.at[:, pl.ds(0, columns)], sems.at[0]),
        pltpu.make_async_copy(partner_ref, held_ref.at[:, pl.ds(columns, columns)], sems.at[1]),
    ]
    for copy in copies:
        copy.start()
    for copy in copies:
        copy.wait()


def hold(own, partner):
    return pl.pallas_call(
        hold_kernel,
        out_shape=pltpu.VMEM((own.shape[0], 2 * own.shape[1]), own.dtype),
        in_specs=[pl.BlockSpec(memory_space=space) for space in (pltpu.HBM, pl.ANY)],
        out_specs=pl.BlockSpec(memory_space=pltpu.VMEM),
        scratch_shapes=[pltpu.SemaphoreType.DMA((2,))],
        compiler_params=pltpu.CompilerParams(vmem_limit_bytes=16 * 1024 * 1024),
        cost_estimate=pl.CostEstimate(
            flops=0, bytes_accessed=2 * 4 * own.size, transcendentals=0
        ),
    )(pltpu.with_memory_space_constraint(own, pltpu.HBM), partner)


def best_of(first, second, held):
    points = jnp.concatenate([first, second], axis=0)
    return jnp.max(jnp.dot(points, held, preferred_element_type=jnp.float32), axis=1)


def place(core, z, y):
    return 64 * core + 8 * (z % 8) + y % 8


def parity_class(core, z_odd, y_odd):
    return [place(core, z, y) for z in range(z_odd, 8, 2) for y in range(y_odd, 8, 2)]


PARITIES = [(0, 0), (0, 1), (1, 0), (1, 1)]


def gather_class(block):
    groups = [parity_class(core, z, y) for core in range(2) for z, y in PARITIES]
    copies = jnp.broadcast_to(block[None], (16,) + block.shape)
    got = lax.all_to_all(copies, COLS, 0, 0, axis_index_groups=groups)
    return got.reshape(-1, block.shape[1])


def from_neighbour(block, z_step, y_step):
    pairs = []
    for core, sign in ((0, 1), (1, -1)):
        for z in range(8):
            for y in range(8):
                source = place(core, z + sign * z_step, y + sign * y_step)
                pairs.append((source, place(core, z, y)))
    return lax.ppermute(block, COLS, pairs)


def merge(tables):
    table = jnp.stack([pair.reshape(2, 128) for pair in tables])
    table = jnp.where(lax.axis_index("z") % 2 == 1, table[::-1], table)
    table = jnp.where(lax.axis_index("y") % 2 == 1, table[:, ::-1], table)
    table = jnp.transpose(table.reshape(2, 2, 4, 4, 2, 4), (2, 0, 3, 1, 4, 5))
    groups = [[place(core, z, y) for z in range(8) for y in range(8)] for core in range(2)]
    shares = lax.all_to_all(table.reshape(64, 2, 4), COLS, 0, 0, axis_index_groups=groups)
    return jnp.max(shares, axis=0)


def swap_pairs(starts):
    return [pair for i in starts for pair in ((i, i + 1), (i + 1, i))]


def rim(patterns):
    odd = lax.axis_index("sx") % 2 == 1
    near = lax.ppermute(patterns, "sx", swap_pairs((0, 2)))
    far = lax.ppermute(patterns, "sx", swap_pairs((1,)))
    above = jnp.where(odd, near[1:], far[1:])
    below = jnp.where(odd, far[:1], near[:1])
    block = jnp.concatenate([above, patterns, below], axis=0)
    even = lax.axis_index(COLS) % 2 == 0
    first, last = block[:, 0:1], block[:, 3:4]
    far = lax.ppermute(jnp.where(even, first, last), COLS, swap_pairs(range(1, 127, 2)))
    near = lax.ppermute(jnp.where(even, last, first), COLS, swap_pairs(range(0, 128, 2)))
    return block, far, near


def valid_weights(weights, rows, cols):
    row = lax.axis_index("sx") * rows + jnp.arange(rows)
    col = lax.axis_index(COLS) * cols + jnp.arange(cols)
    steps = jnp.arange(-1, 2)
    row_near = row[:, None] + steps
    col_near = col[:, None] + steps
    row_valid = (row_near >= 0) & (row_near < rows * lax.axis_size("sx"))
    col_valid = (col_near >= 0) & (col_near < cols * lax.axis_size(COLS))
    valid = row_valid[:, None, :, None] & col_valid[None, :, None, :]
    kept = jnp.where(valid.reshape(rows, cols, 9), jnp.transpose(weights, (1, 2, 0)), 0.0)
    total = jnp.sum(kept, axis=2, keepdims=True)
    even = (lax.axis_index(COLS) % 2 == 0).astype(jnp.float32)
    return jnp.concatenate([kept, total, jnp.full_like(total, even)], axis=2)


def on_device(patterns, nlpar_weights, dictionary):
    rows, cols = patterns.shape[:2]
    partner = lax.ppermute(dictionary, "sy", [(0, 1), (1, 0)])
    weights = valid_weights(nlpar_weights, rows, cols)
    normalized = average(*rim(patterns), weights)
    own = gather_class(normalized)
    ahead = from_neighbour(own, 0, 1)
    across = from_neighbour(own, 1, 0)
    diagonal = from_neighbour(own, 1, 1)
    own, *halves = lax.optimization_barrier((own, dictionary, partner))
    held = hold(*halves)
    early = best_of(own, ahead, held)
    early, across, diagonal = lax.optimization_barrier((early, across, diagonal))
    tables = [early, best_of(across, diagonal, held)]
    return merge(tables)


def solution(mesh):
    split = Mesh(mesh.devices.reshape(4, 2, 8, 8), ("sx",) + COLS)
    return jax.shard_map(
        on_device,
        mesh=split,
        in_specs=(
            P("sx", COLS, None),
            P(None, "sx", COLS),
            P(None, COLS),
        ),
        out_specs=P("sx", COLS),
        check_vma=False,
    )
```

```python
import jax
import jax.numpy as jnp
from jax import lax
from jax.experimental import pallas as pl
from jax.experimental.pallas import tpu as pltpu
from jax.sharding import Mesh
from jax.sharding import PartitionSpec as P

PH = 40
PW = 40
PIX = PH * PW
WIDE = 1792
COLS = ("sy", "z", "y")


def average_kernel(block_ref, far_ref, near_ref, weight_ref, out_ref):
    f32 = jnp.float32
    even = weight_ref[0, 0:1, 10:11] > 0.0
    lines = []
    for row in range(4):
        far, near = far_ref[row].astype(f32), near_ref[row].astype(f32)
        sides = jnp.where(even, far, near), jnp.where(even, near, far)
        lines.append(jnp.concatenate([sides[0], block_ref[row].astype(f32), sides[1]], axis=0))
    averaged = []
    for row in range(2):
        weight = weight_ref[row]
        total = jnp.zeros((4, PIX), f32)
        for row_step in range(3):
            for col_step in range(3):
                index = 3 * row_step + col_step
                near = lines[row + row_step][col_step : col_step + 4]
                total = total + weight[:, index : index + 1] * near
        averaged.append(total / weight[:, 9:10])
    image = jnp.concatenate(averaged, axis=0)
    image = jnp.concatenate([image, jnp.zeros((8, WIDE - PIX), f32)], axis=1)
    pixel = lax.broadcasted_iota(jnp.int32, (8, WIDE), 1)
    column = pixel % PW
    vertical = image
    for offset in (-2, -1, 1, 2):
        vertical = vertical + pltpu.roll(image, (-offset * PW) % WIDE, 1)
    box = vertical
    for offset in (-2, -1, 1, 2):
        inside = (column + offset >= 0) & (column + offset < PW)
        box = box + jnp.where(inside, pltpu.roll(vertical, (-offset) % WIDE, 1), 0.0)
    high = jnp.where(pixel < PIX, image - box / 25.0, 0.0)
    mean = jnp.sum(high, axis=1, keepdims=True) / PIX
    centered = jnp.where(pixel < PIX, high - mean, 0.0)
    scale = jnp.sqrt(jnp.sum(centered * centered, axis=1, keepdims=True) / PIX + 1e-06)
    out_ref[...] = (centered / scale)[:, :PIX].astype(jnp.bfloat16)


def average(block, far, near, weights):
    return pl.pallas_call(
        average_kernel,
        out_shape=jax.ShapeDtypeStruct((8, PIX), jnp.bfloat16),
        in_specs=[pl.BlockSpec(memory_space=pltpu.VMEM)] * 4,
        out_specs=pl.BlockSpec(memory_space=pltpu.VMEM),
        compiler_params=pltpu.CompilerParams(vmem_limit_bytes=16 * 1024 * 1024),
        cost_estimate=pl.CostEstimate(
            flops=100000000000, bytes_accessed=200000, transcendentals=0
        ),
    )(block, far, near, weights)


def hold_kernel(own_ref, partner_ref, held_ref, sems):
    columns = own_ref.shape[1]
    copies = [
        pltpu.make_async_copy(own_ref, held_ref.at[:, pl.ds(0, columns)], sems.at[0]),
        pltpu.make_async_copy(partner_ref, held_ref.at[:, pl.ds(columns, columns)], sems.at[1]),
    ]
    for copy in copies:
        copy.start()
    for copy in copies:
        copy.wait()


def hold(own, partner):
    return pl.pallas_call(
        hold_kernel,
        out_shape=pltpu.VMEM((own.shape[0], 2 * own.shape[1]), own.dtype),
        in_specs=[pl.BlockSpec(memory_space=space) for space in (pltpu.HBM, pl.ANY)],
        out_specs=pl.BlockSpec(memory_space=pltpu.VMEM),
        scratch_shapes=[pltpu.SemaphoreType.DMA((2,))],
        compiler_params=pltpu.CompilerParams(vmem_limit_bytes=16 * 1024 * 1024),
        cost_estimate=pl.CostEstimate(
            flops=0, bytes_accessed=2 * 4 * own.size, transcendentals=0
        ),
    )(pltpu.with_memory_space_constraint(own, pltpu.HBM), partner)


def best_of(points, held):
    return jnp.max(jnp.dot(points, held, preferred_element_type=jnp.float32), axis=1)


def place(core, z, y):
    return 64 * core + 8 * (z % 8) + y % 8


def parity_class(core, z_odd, y_odd):
    return [place(core, z, y) for z in range(z_odd, 8, 2) for y in range(y_odd, 8, 2)]


PARITIES = [(0, 0), (0, 1), (1, 0), (1, 1)]


def gather_class(block):
    groups = [parity_class(core, z, y) for core in range(2) for z, y in PARITIES]
    copies = jnp.broadcast_to(block[None], (16,) + block.shape)
    got = lax.all_to_all(copies, COLS, 0, 0, axis_index_groups=groups)
    return got.reshape(-1, block.shape[1])


def from_neighbour(block, z_step, y_step):
    pairs = []
    for core, sign in ((0, 1), (1, -1)):
        for z in range(8):
            for y in range(8):
                source = place(core, z + sign * z_step, y + sign * y_step)
                pairs.append((source, place(core, z, y)))
    return lax.ppermute(block, COLS, pairs)


def merge(tables):
    table = jnp.stack([pair.reshape(2, 128) for pair in tables])
    table = jnp.where(lax.axis_index("z") % 2 == 1, table[::-1], table)
    table = jnp.where(lax.axis_index("y") % 2 == 1, table[:, ::-1], table)
    table = jnp.transpose(table.reshape(2, 2, 4, 4, 2, 4), (2, 0, 3, 1, 4, 5))
    groups = [[place(core, z, y) for z in range(8) for y in range(8)] for core in range(2)]
    shares = lax.all_to_all(table.reshape(64, 2, 4), COLS, 0, 0, axis_index_groups=groups)
    return jnp.max(shares, axis=0)


def swap_pairs(starts):
    return [pair for i in starts for pair in ((i, i + 1), (i + 1, i))]


def rim(patterns):
    odd = lax.axis_index("sx") % 2 == 1
    near = lax.ppermute(patterns, "sx", swap_pairs((0, 2)))
    far = lax.ppermute(patterns, "sx", swap_pairs((1,)))
    above = jnp.where(odd, near[1:], far[1:])
    below = jnp.where(odd, far[:1], near[:1])
    block = jnp.concatenate([above, patterns, below], axis=0)
    even = lax.axis_index(COLS) % 2 == 0
    first, last = block[:, 0:1], block[:, 3:4]
    far = lax.ppermute(jnp.where(even, first, last), COLS, swap_pairs(range(1, 127, 2)))
    near = lax.ppermute(jnp.where(even, last, first), COLS, swap_pairs(range(0, 128, 2)))
    return block, far, near


def valid_weights(weights, rows, cols):
    row = lax.axis_index("sx") * rows + jnp.arange(rows)
    col = lax.axis_index(COLS) * cols + jnp.arange(cols)
    steps = jnp.arange(-1, 2)
    row_near = row[:, None] + steps
    col_near = col[:, None] + steps
    row_valid = (row_near >= 0) & (row_near < rows * lax.axis_size("sx"))
    col_valid = (col_near >= 0) & (col_near < cols * lax.axis_size(COLS))
    valid = row_valid[:, None, :, None] & col_valid[None, :, None, :]
    kept = jnp.where(valid.reshape(rows, cols, 9), jnp.transpose(weights, (1, 2, 0)), 0.0)
    total = jnp.sum(kept, axis=2, keepdims=True)
    even = (lax.axis_index(COLS) % 2 == 0).astype(jnp.float32)
    return jnp.concatenate([kept, total, jnp.full_like(total, even)], axis=2)


def on_device(patterns, nlpar_weights, dictionary):
    rows, cols = patterns.shape[:2]
    partner = lax.ppermute(dictionary, "sy", [(0, 1), (1, 0)])
    weights = valid_weights(nlpar_weights, rows, cols)
    normalized = average(*rim(patterns), weights)
    own = gather_class(normalized)
    ahead = from_neighbour(own, 0, 1)
    across = from_neighbour(own, 1, 0)
    diagonal = from_neighbour(own, 1, 1)
    own, *halves = lax.optimization_barrier((own, dictionary, partner))
    held = hold(*halves)
    early = best_of(jnp.concatenate([own, ahead], axis=0), held)
    early, diagonal = lax.optimization_barrier((early, diagonal))
    late = best_of(diagonal, held)
    late, across = lax.optimization_barrier((late, across))
    last = best_of(across, held)
    tables = [early, jnp.concatenate([last, late], axis=0)]
    return merge(tables)


def solution(mesh):
    split = Mesh(mesh.devices.reshape(4, 2, 8, 8), ("sx",) + COLS)
    return jax.shard_map(
        on_device,
        mesh=split,
        in_specs=(
            P("sx", COLS, None),
            P(None, "sx", COLS),
            P(None, COLS),
        ),
        out_specs=P("sx", COLS),
        check_vma=False,
    )
```
